32 devices in a mesh: group: 2 (over y), tensor: 4 (over z), dp: 4 (over x, core).
Axes of the slice: x: 2, y: 2, z: 4, core: 2. Of those that a mesh axis runs over, the one named last changes fastest.
Arguments:
- tokens: bfloat16 [1024, 8192], P(('group', 'dp'), 'tensor'), parts along dimension 0, may hold values from -6 to 6
- key_output_gradient: bfloat16 [1024, 1024], P(('group', 'dp'), 'tensor'), parts along dimension 0, may hold values from -6 to 6
- value_output_gradient: bfloat16 [1024, 1024], P(('group', 'dp'), 'tensor'), parts along dimension 0, may hold values from -6 to 6
- frozen_key_weight: bfloat16 [8192, 1024], P(None, 'tensor'), may hold values from -0.09375 to 0.09375
- frozen_value_weight: bfloat16 [8192, 1024], P(None, 'tensor'), may hold values from -0.09375 to 0.09375
- key_down_matrices: bfloat16 [64, 16, 8192], P(None, None, 'tensor'), may hold values from -0.0625 to 0.0625
- value_down_matrices: bfloat16 [64, 16, 8192], P(None, None, 'tensor'), may hold values from -0.0625 to 0.0625
- key_up_matrices: bfloat16 [64, 16, 1024], P(None, None, 'tensor'), may hold values from -0.1875 to 0.1875
- value_up_matrices: bfloat16 [64, 16, 1024], P(None, None, 'tensor'), may hold values from -0.1875 to 0.1875
- segment_length: int32 [8, 16], P(('group', 'dp')), parts along dimension 0, may hold values from 1 to 32, 128 in all within a row
- segment_tenant: int32 [8, 16], P(('group', 'dp')), parts along dimension 0, may hold values from 0 to 63, as said below
- adapter_output_slot: int32 [128], P('group'), parts along dimension 0, may hold values from 0 to 63, as said below
Outputs:
- input_gradient: bfloat16 [1024, 8192], P(('group', 'dp'), 'tensor'), parts along dimension 0
- key_grad_a: float32 [128, 16, 8192], P(('group', 'dp'), None, 'tensor'), parts along dimension 0
- value_grad_a: float32 [128, 16, 8192], P(('group', 'dp'), None, 'tensor'), parts along dimension 0
- key_grad_b: float32 [128, 16, 1024], P(('group', 'dp'), None, 'tensor'), parts along dimension 0
- value_grad_b: float32 [128, 16, 1024], P(('group', 'dp'), None, 'tensor'), parts along dimension 0
The draws below stay inside these ranges and needn't reach their ends.
There are 2 independent parts, one for each index of `group`. The reference program is written for one: setup_inputs(seed, part) draws one part's arguments, and reference() takes and returns one part's arrays. A program takes and returns all parts, laid end to end along the dimension named above; an argument that names none is the same for every part. Nothing has to cross between parts.
Inputs may be any that keep to these rules, and one draw needn't show every extreme that they name: `segment_length`: each row of blocks sums to 128, and its largest entry is 32. `segment_tenant`: call slots q * 16 to (q + 1) * 16 - 1 the range of q. In each block at most 4 segments have tenants whose adapter_output_slot lies in one range, and in every block some range receives exactly 4. `adapter_output_slot`: each of 0 to 63 appears once.
All inputs are finite; a program needn't handle non-finite values.
Results may differ from the reference program's by a relative error of at most 0.013.
Values may be sent and summed in bfloat16 or wider, within the bound.
No kernel may reach another device: no remote copies, remote signals or barrier semaphores. Data moves between devices by JAX's collectives and lax.ppermute only.
A program may use at most 128 MiB of HBM per device.

```python
import math
import jax
import jax.numpy as jnp
import numpy as np
from jax import lax

MODEL_WIDTH = 8192
KEY_VALUE_WIDTH = 1024
ADAPTER_RANK = 16
ADAPTER_TOTAL = 64
SEGS = 16
TOK_DEV = 128
TOKENS = 512
SEG_MOST = 32
EPD = 16
CAP = 4
N_TENSOR = 4
N_DP = 4


def slot_table(key):
    return jax.random.permutation(key, ADAPTER_TOTAL).astype(jnp.int32)


def draw_adapter_output_slot(key, part):
    return slot_table(key)


def draw_segment_tenant(key, part):
    table = slot_table(key)
    key = jax.random.fold_in(key, 11)
    inverse = jnp.argsort(table).astype(jnp.int32)
    spill_size = (SEGS - CAP + N_DP - 2) // (N_DP - 1)
    seg_index = jnp.arange(SEGS, dtype=jnp.int32)
    owner_rank = jnp.where(seg_index < CAP, 0, 1 + (seg_index - CAP) // spill_size)

    def one_block(key_of_block):
        key_owner, key_order, key_within = jax.random.split(key_of_block, 3)
        owners = jax.random.permutation(key_owner, N_DP).astype(jnp.int32)[owner_rank]
        owners = owners[jax.random.permutation(key_order, SEGS)]
        within = jax.random.randint(key_within, (SEGS,), 0, EPD).astype(jnp.int32)
        return inverse[owners * EPD + within]
    return jax.vmap(one_block)(jax.random.split(key, N_DP)).astype(jnp.int32)


def with_spikes(result, key, source, target, shards_of, factor):
    owner, partner = [(jnp.arange(result.shape[axis_at]) // (result.shape[axis_at] // shards_of)).reshape([-1 if axis == axis_at else 1 for axis in range(result.ndim)]) for axis_at in (source, target)]
    chosen = jax.random.permutation(key, shards_of)[partner]
    strong = (owner == chosen) | (owner == (partner + shards_of // 2) % shards_of)
    return jnp.where(strong, factor * result, result)


def level_of(key, dims, shards, smallest, largest):
    loudness, own = 1.0, jax.random.fold_in(key, 6)
    for dim, parts in shards:
        steps = jnp.exp(jax.random.uniform(jax.random.fold_in(own, dim), (parts,), jnp.float32, smallest / len(shards), largest / len(shards)))
        loudness = loudness * jnp.repeat(steps, dims[dim] // parts).reshape([-1 if axis == dim else 1 for axis in range(len(dims))])
    return loudness


def split_up(number_of, total, bound, skew):
    weights = [(1 << 20) // math.isqrt(grade ** skew) + 1 for grade in range(2, number_of + 1)]
    surplus, holding = total - bound - (number_of - 1), [1] * (number_of - 1)
    while surplus > 0:
        candidates = [i for i in range(number_of - 1) if holding[i] < bound]
        mass, budget = sum([weights[i] for i in candidates]), surplus
        for i in candidates:
            addition = min(bound - holding[i], max(1, budget * weights[i] // mass), surplus)
            holding[i] = holding[i] + addition
            surplus = surplus - addition
    return np.array([bound] + holding)


def uneven_parts(rng, amount, total, limit, lean):
    if amount == 2:
        one = jax.random.randint(rng, (), max(1, total - limit), min(limit, total - 1) + 1)
        return jnp.stack([one, total - one])
    lengths = jnp.asarray(split_up(amount, total, limit, lean), jnp.int32)
    pairs = (amount - 1) // 2
    donor, sink = lengths[1:1 + 2 * pairs:2], lengths[2:2 + 2 * pairs:2]
    slack = jnp.minimum(donor - 1, limit - sink)
    moved = jax.random.randint(jax.random.fold_in(rng, 1), (pairs,), 0, 1 << 20) % (slack + 1)
    lengths = lengths.at[1:1 + 2 * pairs:2].set(donor - moved).at[2:2 + 2 * pairs:2].set(sink + moved)
    return lengths[jax.random.permutation(jax.random.fold_in(rng, 2), amount)]


def gaussian(rng, dims, width, bound, cuts=(), kind=jnp.bfloat16):
    array = jax.random.normal(rng, dims, jnp.float32) * width
    if len(cuts) > 0:
        array = level_of(rng, dims, cuts, -0.22, 0.18) * array
    return jnp.clip(array, min=-bound, max=bound).astype(kind)


def gaussian_with(own_key, shape, deviation, reach, cuts, heavy, kind=jnp.bfloat16):
    drawn = deviation * jax.random.normal(own_key, shape, jnp.float32)
    if cuts:
        drawn = drawn * level_of(own_key, shape, cuts, -0.22, 0.18)
    return jnp.clip(with_spikes(drawn, jax.random.fold_in(own_key, 3), *heavy), -reach, reach).astype(kind)


def setup_inputs(seed: int = 0, part: int = 0) -> dict:
    seeds = jax.random.split(jax.random.key(seed), 13)
    own_keys = jax.random.split(jax.random.fold_in(seeds[12], part), 13)
    return {
        "tokens": gaussian(own_keys[0], (TOKENS, MODEL_WIDTH), 1.0, 6.0, ((0, 4), (1, 4))),
        "key_output_gradient": gaussian(own_keys[1], (TOKENS, KEY_VALUE_WIDTH), 1.0, 6.0, ((0, 4), (1, 4))),
        "value_output_gradient": gaussian(own_keys[2], (TOKENS, KEY_VALUE_WIDTH), 1.0, 6.0, ((0, 4), (1, 4))),
        "frozen_key_weight": gaussian_with(seeds[3], (MODEL_WIDTH, KEY_VALUE_WIDTH), MODEL_WIDTH ** -0.5, 0.09375, ((1, 4),), (1, 0, 4, 2.0)),
        "frozen_value_weight": gaussian_with(seeds[4], (MODEL_WIDTH, KEY_VALUE_WIDTH), MODEL_WIDTH ** -0.5, 0.09375, ((1, 4),), (1, 0, 4, 2.0)),
        "key_down_matrices": gaussian(seeds[5], (ADAPTER_TOTAL, ADAPTER_RANK, MODEL_WIDTH), MODEL_WIDTH ** -0.5, 0.0625, ((2, 4),)),
        "value_down_matrices": gaussian(seeds[6], (ADAPTER_TOTAL, ADAPTER_RANK, MODEL_WIDTH), MODEL_WIDTH ** -0.5, 0.0625, ((2, 4),)),
        "key_up_matrices": gaussian(seeds[7], (ADAPTER_TOTAL, ADAPTER_RANK, KEY_VALUE_WIDTH), KEY_VALUE_WIDTH ** -0.5, 0.1875, ((2, 4),)),
        "value_up_matrices": gaussian(seeds[8], (ADAPTER_TOTAL, ADAPTER_RANK, KEY_VALUE_WIDTH), KEY_VALUE_WIDTH ** -0.5, 0.1875, ((2, 4),)),
        "segment_length": jax.vmap(lambda own: uneven_parts(own, SEGS, TOK_DEV, SEG_MOST, 2))(jax.random.split(own_keys[9], N_DP)).reshape((N_DP, SEGS)).astype(jnp.int32),
        "segment_tenant": draw_segment_tenant(jax.random.fold_in(jax.random.fold_in(seeds[12], part), 71), part),
        "adapter_output_slot": draw_adapter_output_slot(jax.random.fold_in(jax.random.fold_in(seeds[12], part), 71), part),
    }


ADAPTER_SCALE = 2.0
LOSS_UNSCALE = 0.125


def block_products(tokens, key_output_gradient, value_output_gradient, frozen_key_weight, frozen_value_weight, key_down_matrices, value_down_matrices, key_up_matrices, value_up_matrices, segment_lengths, tenant_list):
    row_count = tokens.shape[0]
    segment_count = tenant_list.shape[0]
    seg_ends = jnp.cumsum(segment_lengths).astype(jnp.int32)
    starts = seg_ends - segment_lengths
    position = jnp.arange(row_count, dtype=jnp.int32)[:, None]
    member = ((position >= starts[None, :]) & (position < seg_ends[None, :])).astype(jnp.float32)

    def collapse(values):
        return jnp.sum(values.reshape(row_count, segment_count, ADAPTER_RANK) * member[:, :, None], axis=1)

    def spread_rows(values):
        widened = member[:, :, None] * values.astype(jnp.float32)[:, None, :]
        return widened.reshape(row_count, segment_count * ADAPTER_RANK).astype(jnp.bfloat16)

    key_down_rows = key_down_matrices[tenant_list].reshape(segment_count * ADAPTER_RANK, MODEL_WIDTH)
    value_down_rows = value_down_matrices[tenant_list].reshape(segment_count * ADAPTER_RANK, MODEL_WIDTH)
    key_up_rows = key_up_matrices[tenant_list].reshape(segment_count * ADAPTER_RANK, KEY_VALUE_WIDTH)
    value_up_rows = value_up_matrices[tenant_list].reshape(segment_count * ADAPTER_RANK, KEY_VALUE_WIDTH)
    key_down_gradient = collapse(jnp.dot(tokens, key_down_rows.T, preferred_element_type=jnp.float32)).astype(jnp.bfloat16)
    value_down_gradient = collapse(jnp.dot(tokens, value_down_rows.T, preferred_element_type=jnp.float32)).astype(jnp.bfloat16)
    back_key = collapse(jnp.dot(key_output_gradient, key_up_rows.T, preferred_element_type=jnp.float32)).astype(jnp.bfloat16)
    back_value = collapse(jnp.dot(value_output_gradient, value_up_rows.T, preferred_element_type=jnp.float32)).astype(jnp.bfloat16)
    col_width = KEY_VALUE_WIDTH // N_TENSOR

    def add_group(total, group):
        start = (group * col_width).astype(jnp.int32)
        gk = lax.dynamic_slice_in_dim(key_output_gradient, start, col_width, 1)
        gv = lax.dynamic_slice_in_dim(value_output_gradient, start, col_width, 1)
        wk = lax.dynamic_slice_in_dim(frozen_key_weight, start, col_width, 1)
        wv = lax.dynamic_slice_in_dim(frozen_value_weight, start, col_width, 1)
        term = jnp.dot(gk, wk.T, preferred_element_type=jnp.float32) + jnp.dot(gv, wv.T, preferred_element_type=jnp.float32)
        rounded = lax.optimization_barrier(term.astype(jnp.bfloat16))
        return total + rounded.astype(jnp.float32), None

    frozen_gradient, _ = lax.scan(add_group, jnp.zeros((row_count, MODEL_WIDTH), jnp.float32), jnp.arange(N_TENSOR, dtype=jnp.int32))
    key_back_spread = spread_rows(back_key)
    value_back_spread = spread_rows(back_value)
    local_adapter = jnp.dot(key_back_spread, key_down_rows, preferred_element_type=jnp.float32) + jnp.dot(value_back_spread, value_down_rows, preferred_element_type=jnp.float32)
    input_gradient = (frozen_gradient + ADAPTER_SCALE * local_adapter).astype(jnp.bfloat16)
    key_down_partial = ADAPTER_SCALE * jnp.dot(key_back_spread.T, tokens, preferred_element_type=jnp.float32).reshape(segment_count, ADAPTER_RANK, MODEL_WIDTH)
    value_down_partial = ADAPTER_SCALE * jnp.dot(value_back_spread.T, tokens, preferred_element_type=jnp.float32).reshape(segment_count, ADAPTER_RANK, MODEL_WIDTH)
    key_up_partial = ADAPTER_SCALE * jnp.dot(spread_rows(key_down_gradient).T, key_output_gradient, preferred_element_type=jnp.float32).reshape(segment_count, ADAPTER_RANK, KEY_VALUE_WIDTH)
    value_up_partial = ADAPTER_SCALE * jnp.dot(spread_rows(value_down_gradient).T, value_output_gradient, preferred_element_type=jnp.float32).reshape(segment_count, ADAPTER_RANK, KEY_VALUE_WIDTH)
    return input_gradient, key_down_partial, value_down_partial, key_up_partial, value_up_partial


def reference(tokens, key_output_gradient, value_output_gradient, frozen_key_weight, frozen_value_weight, key_down_matrices, value_down_matrices, key_up_matrices, value_up_matrices, segment_length, segment_tenant, adapter_output_slot):
    blocks = segment_length.shape[0]

    def one_block(inputs):
        token_block, key_of_block, value_of_block, segment_lengths, tenant_list = inputs
        return block_products(token_block, key_of_block, value_of_block, frozen_key_weight, frozen_value_weight, key_down_matrices, value_down_matrices, key_up_matrices, value_up_matrices, segment_lengths, tenant_list)

    outputs = lax.map(one_block, (tokens.reshape(blocks, TOK_DEV, MODEL_WIDTH), key_output_gradient.reshape(blocks, TOK_DEV, KEY_VALUE_WIDTH), value_output_gradient.reshape(blocks, TOK_DEV, KEY_VALUE_WIDTH), segment_length, segment_tenant))
    input_gradient = outputs[0].reshape(blocks * TOK_DEV, MODEL_WIDTH)
    target = adapter_output_slot[segment_tenant.reshape(-1)].astype(jnp.int32)
    key_grad_a = LOSS_UNSCALE * jax.ops.segment_sum(outputs[1].reshape(-1, ADAPTER_RANK, MODEL_WIDTH), target, num_segments=ADAPTER_TOTAL)
    value_grad_a = LOSS_UNSCALE * jax.ops.segment_sum(outputs[2].reshape(-1, ADAPTER_RANK, MODEL_WIDTH), target, num_segments=ADAPTER_TOTAL)
    key_grad_b = LOSS_UNSCALE * jax.ops.segment_sum(outputs[3].reshape(-1, ADAPTER_RANK, KEY_VALUE_WIDTH), target, num_segments=ADAPTER_TOTAL)
    value_grad_b = LOSS_UNSCALE * jax.ops.segment_sum(outputs[4].reshape(-1, ADAPTER_RANK, KEY_VALUE_WIDTH), target, num_segments=ADAPTER_TOTAL)
    return (input_gradient, key_grad_a, value_grad_a, key_grad_b, value_grad_b)
```

```python
import functools

import jax
import jax.numpy as jnp
from jax import lax
from jax.experimental import pallas as pl
from jax.experimental.pallas import tpu as pltpu
from jax.sharding import PartitionSpec as P

ADAPTER_SCALE = 2.0
LOSS_UNSCALE = 0.125
VMEM_BYTES = 48 * 1024 * 1024
SLOT_ROWS = 16

f32 = jnp.float32
bf16 = jnp.bfloat16


def dot_nt(former, latter):
    return lax.dot_general(former, latter, (((1,), (1,)), ((), ())), preferred_element_type=f32)


def dot_nn(former, latter):
    return lax.dot_general(former, latter, (((1,), (0,)), ((), ())), preferred_element_type=f32)


def dot_tn(former, latter):
    return lax.dot_general(former, latter, (((0,), (0,)), ((), ())), preferred_element_type=f32)


def params():
    return pltpu.CompilerParams(vmem_limit_bytes=VMEM_BYTES)


def frozen_kernel(block_ref, gk_ref, gv_ref, wk_ref, wv_ref, out_ref):
    del block_ref
    value = dot_nt(gk_ref[...], wk_ref[...]) + dot_nt(gv_ref[...], wv_ref[...])
    out_ref[...] = value.astype(out_ref.dtype)


def frozen_block(block, gk, gv, wk, wv, width, dtype, steps=4):
    rows, feats = gk.shape
    part = width // steps
    return pl.pallas_call(
        frozen_kernel,
        grid_spec=pltpu.PrefetchScalarGridSpec(
            num_scalar_prefetch=1,
            grid=(steps,),
            in_specs=[
                pl.BlockSpec((rows, feats), lambda i, b: (0, 0)),
                pl.BlockSpec((rows, feats), lambda i, b: (0, 0)),
                pl.BlockSpec((part, feats), lambda i, b: (b[0] * steps + i, 0)),
                pl.BlockSpec((part, feats), lambda i, b: (b[0] * steps + i, 0)),
            ],
            out_specs=pl.BlockSpec((rows, part), lambda i, b: (0, i)),
        ),
        out_shape=jax.ShapeDtypeStruct((rows, width), dtype),
        compiler_params=params(),
        cost_estimate=pl.CostEstimate(
            flops=4 * rows * feats * width, bytes_accessed=4 * feats * width, transcendentals=0
        ),
        name="frozen_block",
    )(block, gk, gv, wk, wv)


def segment_masks(len_ref, rows, segments, rank):
    shape = (segments * rank, rows)
    row = lax.broadcasted_iota(jnp.int32, shape, 1)
    seg = lax.broadcasted_iota(jnp.int32, shape, 0) // rank
    start = jnp.zeros(shape, jnp.int32)
    end = jnp.zeros(shape, jnp.int32)
    total = jnp.int32(0)
    for k in range(segments):
        begin = total
        total = total + len_ref[0, k]
        start = jnp.where(seg == k, begin, start)
        end = jnp.where(seg == k, total, end)
    return (row >= start) & (row < end)


def lowrank_kernel(
    len_ref, tenant_ref, slot_ref, tok_hbm, gk_hbm, gv_hbm, kd_hbm, vd_hbm, ku_hbm, vu_hbm,
    out_ref, tok, gk, gv, down, up, sems,
):
    segments = tenant_ref.shape[1]
    rank = kd_hbm.shape[1]
    rows = tok.shape[0]
    half = segments * rank
    copies = [
        pltpu.make_async_copy(tok_hbm, tok, sems.at[0, 0]),
        pltpu.make_async_copy(gk_hbm, gk, sems.at[0, 1]),
        pltpu.make_async_copy(gv_hbm, gv, sems.at[0, 2]),
    ]
    for k in range(segments):
        tenant = tenant_ref[0, k]
        at = pl.ds(k * rank, rank)
        after = pl.ds(half + k * rank, rank)
        copies.append(pltpu.make_async_copy(kd_hbm.at[tenant], down.at[at], sems.at[1, k]))
        copies.append(pltpu.make_async_copy(vd_hbm.at[tenant], down.at[after], sems.at[2, k]))
        copies.append(pltpu.make_async_copy(ku_hbm.at[tenant], up.at[at], sems.at[3, k]))
        copies.append(pltpu.make_async_copy(vu_hbm.at[tenant], up.at[after], sems.at[4, k]))
    for copy in copies:
        copy.start()
    mask = segment_masks(len_ref, rows, segments, rank)
    slot_of = jnp.zeros((SLOT_ROWS, rows), f32)
    position = lax.broadcasted_iota(jnp.int32, (SLOT_ROWS, rows), 1)
    total = jnp.int32(0)
    for k in range(segments):
        begin = total
        total = total + len_ref[0, k]
        slot = slot_ref[tenant_ref[0, k]].astype(f32)
        slot_of = jnp.where((position >= begin) & (position < total), slot, slot_of)
    out_ref[4 * rank :, :] = slot_of.astype(bf16)
    for copy in copies:
        copy.wait()

    def fold(values):
        kept = jnp.where(mask, values, 0.0)
        return jnp.sum(kept.reshape(segments, rank, rows), axis=0).astype(bf16)

    out_ref[0:rank, :] = fold(dot_nt(down[:half], tok[...]))
    out_ref[rank : 2 * rank, :] = fold(dot_nt(down[half:], tok[...]))
    out_ref[2 * rank : 3 * rank, :] = fold(dot_nt(up[:half], gk[...]))
    out_ref[3 * rank : 4 * rank, :] = fold(dot_nt(up[half:], gv[...]))


def lowrank(tokens, gk, gv, kd, vd, ku, vu, lengths, tenants, slots):
    rows, width = tokens.shape
    feats = gk.shape[1]
    segments = tenants.shape[1]
    rank = kd.shape[1]
    both = 2 * segments * rank
    smem = pl.BlockSpec(memory_space=pltpu.SMEM)
    anywhere = pl.BlockSpec(memory_space=pl.ANY)
    return pl.pallas_call(
        lowrank_kernel,
        in_specs=[smem] * 3 + [anywhere] * 7,
        out_specs=pl.BlockSpec(memory_space=pltpu.VMEM),
        out_shape=jax.ShapeDtypeStruct((4 * rank + SLOT_ROWS, rows), bf16),
        scratch_shapes=[
            pltpu.VMEM((rows, width), bf16),
            pltpu.VMEM((rows, feats), bf16),
            pltpu.VMEM((rows, feats), bf16),
            pltpu.VMEM((both, width), bf16),
            pltpu.VMEM((both, feats), bf16),
            pltpu.SemaphoreType.DMA((5, segments)),
        ],
        compiler_params=params(),
        cost_estimate=pl.CostEstimate(
            flops=2 * rows * both * (width + feats),
            bytes_accessed=2 * (rows + both) * (width + feats),
            transcendentals=0,
        ),
        name="lowrank",
    )(lengths, tenants, slots, tokens, gk, gv, kd, vd, ku, vu)


def own_kernel(
    len_ref, tenant_ref, z_ref, gk_ref, gv_ref, sums_ref, wk_hbm, wv_hbm, kd_hbm, vd_hbm,
    out_ref, wk, wv, down, sems,
):
    segments = tenant_ref.shape[1]
    rank = kd_hbm.shape[1]
    rows, width = out_ref.shape
    half = segments * rank
    block = pl.ds(pl.multiple_of(z_ref[0] * width, width), width)
    copies = [
        pltpu.make_async_copy(wk_hbm.at[block], wk, sems.at[0, 0]),
        pltpu.make_async_copy(wv_hbm.at[block], wv, sems.at[0, 1]),
    ]
    for k in range(segments):
        tenant = tenant_ref[0, k]
        at = pl.ds(k * rank, rank)
        after = pl.ds(half + k * rank, rank)
        copies.append(pltpu.make_async_copy(kd_hbm.at[tenant], down.at[at], sems.at[1, k]))
        copies.append(pltpu.make_async_copy(vd_hbm.at[tenant], down.at[after], sems.at[2, k]))
    for copy in copies:
        copy.start()
    mask = segment_masks(len_ref, rows, segments, rank)

    def spread(first):
        values = sums_ref[first : first + rank, :].astype(f32)
        tiled = jnp.concatenate([values] * segments, axis=0)
        return jnp.where(mask, ADAPTER_SCALE * tiled, 0.0).astype(bf16)

    back = jnp.concatenate([spread(2 * rank), spread(3 * rank)], axis=0)
    for copy in copies:
        copy.wait()
    out_ref[...] = (
        dot_nt(gk_ref[...], wk[...]) + dot_nt(gv_ref[...], wv[...]) + dot_tn(back, down[...])
    )


def own_columns(z, gk, gv, sums, wk, wv, kd, vd, lengths, tenants):
    rows, feats = gk.shape
    width = kd.shape[2]
    segments = tenants.shape[1]
    rank = kd.shape[1]
    both = 2 * segments * rank
    smem = pl.BlockSpec(memory_space=pltpu.SMEM)
    vmem = pl.BlockSpec(memory_space=pltpu.VMEM)
    anywhere = pl.BlockSpec(memory_space=pl.ANY)
    return pl.pallas_call(
        own_kernel,
        in_specs=[smem] * 3 + [vmem] * 3 + [anywhere] * 4,
        out_specs=vmem,
        out_shape=jax.ShapeDtypeStruct((rows, width), f32),
        scratch_shapes=[
            pltpu.VMEM((width, feats), bf16),
            pltpu.VMEM((width, feats), bf16),
            pltpu.VMEM((both, width), bf16),
            pltpu.SemaphoreType.DMA((3, segments)),
        ],
        compiler_params=params(),
        cost_estimate=pl.CostEstimate(
            flops=2 * rows * width * (2 * feats + both),
            bytes_accessed=2 * width * (2 * feats + both + 2 * rows),
            transcendentals=0,
        ),
        name="own_columns",
    )(lengths, tenants, z, gk, gv, sums, wk, wv, kd, vd)


def grads_kernel(count, rank, per_owner, first_ref, *refs):
    sums = refs[:count]
    chunks = refs[count : 2 * count]
    ends = refs[2 * count : 3 * count]
    ka_ref, va_ref, kb_ref, vb_ref, spread_ref = refs[3 * count :]
    size = per_owner * rank
    scale = ADAPTER_SCALE * LOSS_UNSCALE

    @pl.when(pl.program_id(0) == 0)
    def _():
        feats = kb_ref.shape[2]
        rows = sums[0].shape[1]
        wanted = lax.broadcasted_iota(jnp.int32, (size, rows), 0) // rank + first_ref[0]
        b_key = jnp.zeros((size, feats), f32)
        b_value = jnp.zeros((size, feats), f32)
        for n in range(count):
            slot = sums[n][4 * rank : 4 * rank + 1, :].astype(f32).astype(jnp.int32)
            mask = wanted == slot

            def spread(index):
                values = sums[n][index * rank : (index + 1) * rank, :].astype(f32)
                tiled = jnp.concatenate([values] * per_owner, axis=0)
                return jnp.where(mask, tiled, 0.0).astype(bf16)

            columns = slice(n * rows, (n + 1) * rows)
            spread_ref[0:size, columns] = spread(2)
            spread_ref[size:, columns] = spread(3)
            b_key += dot_nn(spread(0), ends[n][:, :feats])
            b_value += dot_nn(spread(1), ends[n][:, feats:])
        kb_ref[...] = (scale * b_key).reshape(kb_ref.shape)
        vb_ref[...] = (scale * b_value).reshape(vb_ref.shape)

    tokens = jnp.concatenate([chunk[...] for chunk in chunks], axis=0)
    product = scale * dot_nn(spread_ref[...], tokens)
    ka_ref[...] = product[:size].reshape(ka_ref.shape)
    va_ref[...] = product[size:].reshape(va_ref.shape)


def adapter_grads(first, sums, sent, rank, per_owner, width, feats):
    count = len(sums)
    rows = sent[0].shape[0]
    chunk = 2 * feats
    steps = width // chunk
    a_spec = pl.BlockSpec((per_owner, rank, chunk), lambda i: (0, 0, i))
    b_spec = pl.BlockSpec((per_owner, rank, feats), lambda i: (0, 0, 0))
    return pl.pallas_call(
        functools.partial(grads_kernel, count, rank, per_owner),
        grid=(steps,),
        in_specs=[pl.BlockSpec(memory_space=pltpu.SMEM)]
        + [pl.BlockSpec(sums[0].shape, lambda i: (0, 0))] * count
        + [pl.BlockSpec((rows, chunk), lambda i: (0, i))] * count
        + [pl.BlockSpec((rows, chunk), lambda i: (0, steps))] * count,
        out_specs=[a_spec, a_spec, b_spec, b_spec],
        out_shape=[
            jax.ShapeDtypeStruct((per_owner, rank, width), f32),
            jax.ShapeDtypeStruct((per_owner, rank, width), f32),
            jax.ShapeDtypeStruct((per_owner, rank, feats), f32),
            jax.ShapeDtypeStruct((per_owner, rank, feats), f32),
        ],
        scratch_shapes=[pltpu.VMEM((2 * per_owner * rank, count * rows), bf16)],
        compiler_params=params(),
        cost_estimate=pl.CostEstimate(
            flops=4 * per_owner * rank * count * rows * (width + feats),
            bytes_accessed=8 * per_owner * rank * (width + feats) + 2 * count * rows * width,
            transcendentals=0,
        ),
        name="adapter_grads",
    )(first, *sums, *sent, *sent)


def swap(values, axis, bit, size):
    return lax.ppermute(values, axis, [(i, i ^ bit) for i in range(size)])


def local(
    tokens, gk, gv, wk, wv, kd, vd, ku, vu, segment_length, segment_tenant, adapter_output_slot
):
    rows, width = tokens.shape
    feats = gk.shape[1]
    adapters, rank, _ = kd.shape
    n_tensor = lax.axis_size("tensor")
    n_dp = lax.axis_size("dp")
    per_owner = adapters // n_dp
    z = lax.axis_index("tensor")
    first = (lax.axis_index("dp") * per_owner).astype(jnp.int32).reshape(1)
    z_index = z.astype(jnp.int32).reshape(1)

    sent = jnp.concatenate([tokens, gk, gv], axis=1)

    if n_tensor == 4:
        odd = z_index % 2
        edge = (z_index == 0) | (z_index == 3)
        x0 = frozen_block(jnp.where(odd == 1, 0, 3), gk, gv, wk, wv, width, bf16)
        r1 = swap(x0, "tensor", 1, 4)
        x1 = frozen_block(jnp.where(odd == 1, 2, 1), gk, gv, wk, wv, width, bf16)
        r2 = lax.ppermute(x1, "tensor", [(1, 2), (2, 1)])
        r4 = lax.ppermute(x1, "tensor", [(0, 1), (3, 2)])
        x2 = frozen_block(z_index ^ 2, gk, gv, wk, wv, width, f32)
        x2 = jnp.where(edge[0], x2, x2 + r1.astype(f32)).astype(bf16)
        r3 = swap(x2, "tensor", 2, 4)

    part = lowrank(
        tokens, gk, gv, kd, vd, ku, vu, segment_length, segment_tenant, adapter_output_slot
    )
    products, slot_rows = part[: 4 * rank], part[4 * rank :]
    if n_tensor == 4:
        total = products.astype(f32)
        for bit in (1, 2, 3):
            total = total + swap(products, "tensor", bit, 4).astype(f32)
    else:
        total = lax.psum(products.astype(f32), "tensor")
    sums = jnp.concatenate([total.astype(bf16), slot_rows], axis=0)

    if n_dp == 4:
        across = swap(sent, "dp", 2, 4)
        all_sent = [sent, across, swap(sent, "dp", 1, 4), swap(across, "dp", 1, 4)]
        across = swap(sums, "dp", 2, 4)
        all_sums = [sums, across, swap(sums, "dp", 1, 4), swap(across, "dp", 1, 4)]
    else:
        gathered = lax.all_gather(sent, "dp")
        all_sent = [gathered[i] for i in range(n_dp)]
        gathered = lax.all_gather(sums, "dp")
        all_sums = [gathered[i] for i in range(n_dp)]

    own = own_columns(
        z_index, gk, gv, sums, wk, wv, kd, vd, segment_length, segment_tenant
    )
    if n_tensor == 4:
        near = r2.astype(f32) + r4.astype(f32)
        own = own + jnp.where(edge[0], r1.astype(f32), near)
        input_gradient = (own + r3.astype(f32)).astype(bf16)
    else:
        blocks = [
            frozen_block(jnp.full((1,), b, jnp.int32), gk, gv, wk, wv, width, bf16)
            for b in range(n_tensor)
        ]
        mine = lax.psum_scatter(
            jnp.concatenate(blocks, axis=1), "tensor", scatter_dimension=1, tiled=True
        )
        term = frozen_block(z_index, gk, gv, wk, wv, width, f32)
        input_gradient = (own - term + mine.astype(f32)).astype(bf16)

    grads = adapter_grads(first, all_sums, all_sent, rank, per_owner, width, feats)
    return (input_gradient, *grads)


def solution(mesh):
    placed = (
        P(("group", "dp"), "tensor"),
        P(("group", "dp"), "tensor"),
        P(("group", "dp"), "tensor"),
        P(None, "tensor"),
        P(None, "tensor"),
        P(None, None, "tensor"),
        P(None, None, "tensor"),
        P(None, None, "tensor"),
        P(None, None, "tensor"),
        P(("group", "dp"), None),
        P(("group", "dp"), None),
        P("group"),
    )
    return jax.shard_map(
        local,
        mesh=mesh,
        in_specs=placed,
        out_specs=(
            P(("group", "dp"), "tensor"),
            P(("group", "dp"), None, "tensor"),
            P(("group", "dp"), None, "tensor"),
            P(("group", "dp"), None, "tensor"),
            P(("group", "dp"), None, "tensor"),
        ),
        check_vma=False,
    )
```

```python
import functools

import jax
import jax.numpy as jnp
from jax import lax
from jax.experimental import pallas as pl
from jax.experimental.pallas import tpu as pltpu
from jax.sharding import PartitionSpec as P

ADAPTER_SCALE = 2.0
LOSS_UNSCALE = 0.125
VMEM_BYTES = 48 * 1024 * 1024
COST = pl.CostEstimate(flops=0, bytes_accessed=0, transcendentals=0)

f32 = jnp.float32
bf16 = jnp.bfloat16


def dot_nt(former, latter):
    return lax.dot_general(former, latter, (((1,), (1,)), ((), ())), preferred_element_type=f32)


def dot_nn(former, latter):
    return lax.dot_general(former, latter, (((1,), (0,)), ((), ())), preferred_element_type=f32)


def dot_tn(former, latter):
    return lax.dot_general(former, latter, (((0,), (0,)), ((), ())), preferred_element_type=f32)


def params():
    return pltpu.CompilerParams(vmem_limit_bytes=VMEM_BYTES)


def frozen_part(gk, gv, wk, wv):
    return dot_nt(gk, wk) + dot_nt(gv, wv)


def frozen_copies(block, width, wk_hbm, wv_hbm, wk, wv, sems):
    rows = pl.ds(pl.multiple_of(block * width, width), width)
    return [
        pltpu.make_async_copy(wk_hbm.at[rows], wk, sems.at[0]),
        pltpu.make_async_copy(wv_hbm.at[rows], wv, sems.at[1]),
    ]


def frozen_kernel(gk_hbm, gv_hbm, wk_hbm, wv_hbm, *refs):
    *outs, gk, gv, wk, wv, sems = refs
    width = outs[0].shape[1]
    z = lax.axis_index("tensor")
    head = [
        pltpu.make_async_copy(gk_hbm, gk, sems.at[len(outs), 0]),
        pltpu.make_async_copy(gv_hbm, gv, sems.at[len(outs), 1]),
    ]
    body = [
        frozen_copies(block, width, wk_hbm, wv_hbm, wk.at[n], wv.at[n], sems.at[n])
        for n, block in enumerate((z ^ 2, z ^ 1, z))
    ]
    for copies in (head, *body):
        for copy in copies:
            copy.start()
    for copy in head:
        copy.wait()
    for n, out in enumerate(outs):
        for copy in body[n]:
            copy.wait()
        out[...] = frozen_part(gk[...], gv[...], wk[n], wv[n]).astype(out.dtype)


def frozen_blocks(gk, gv, wk, wv, width, dtypes):
    rows, feats = gk.shape
    count = len(dtypes)
    hbm = pl.BlockSpec(memory_space=pltpu.HBM)
    vmem = pl.BlockSpec(memory_space=pltpu.VMEM)
    return pl.pallas_call(
        frozen_kernel,
        in_specs=[hbm] * 4,
        out_specs=[vmem] * count,
        out_shape=[jax.ShapeDtypeStruct((rows, width), dtype) for dtype in dtypes],
        scratch_shapes=[
            pltpu.VMEM((rows, feats), bf16),
            pltpu.VMEM((rows, feats), bf16),
            pltpu.VMEM((count, width, feats), bf16),
            pltpu.VMEM((count, width, feats), bf16),
            pltpu.SemaphoreType.DMA((count + 1, 2)),
        ],
        compiler_params=params(),
        cost_estimate=COST,
        name="frozen_blocks",
    )(gk, gv, wk, wv)


def segment_masks(len_ref, shape, segments):
    position = lax.broadcasted_iota(jnp.int32, shape, 1)
    masks = []
    total = jnp.int32(0)
    for k in range(segments):
        begin = total
        total = total + len_ref[0, k]
        masks.append((position >= begin) & (position < total))
    return masks


def first_kernel(
    frozen, len_hbm, tenant_hbm, slot_hbm, tok_hbm, gk_hbm, gv_hbm, kd_hbm, vd_hbm, ku_hbm, vu_hbm,
    wk_hbm, wv_hbm, out_ref, term_ref, len_ref, tenant_ref, slot_ref, tok, gk, gv, down, key_up,
    value_up, wk, wv, products, sems,
):
    segments = tenant_ref.shape[1]
    rank = kd_hbm.shape[1]
    rows, width = tok.shape
    half = segments * rank
    scalars = [
        pltpu.make_async_copy(tenant_hbm, tenant_ref, sems.at[0, 0]),
        pltpu.make_async_copy(len_hbm, len_ref, sems.at[0, 1]),
        pltpu.make_async_copy(slot_hbm, slot_ref, sems.at[0, 2]),
    ]
    grads = [
        pltpu.make_async_copy(gk_hbm, gk, sems.at[0, 3]),
        pltpu.make_async_copy(gv_hbm, gv, sems.at[0, 4]),
    ]
    weights = []
    if frozen:
        weights = frozen_copies(
            lax.axis_index("tensor") ^ 3, width, wk_hbm, wv_hbm, wk, wv, sems.at[3]
        )
    ups = [
        pltpu.make_async_copy(ku_hbm, key_up, sems.at[0, 5]),
        pltpu.make_async_copy(vu_hbm, value_up, sems.at[0, 6]),
    ]
    downs = [pltpu.make_async_copy(tok_hbm, tok, sems.at[0, 7])]
    for copy in scalars + grads + weights + ups + downs:
        copy.start()
    for copy in scalars:
        copy.wait()
    for k in range(segments):
        tenant = tenant_ref[0, k]
        at = pl.ds(k * rank, rank)
        after = pl.ds(half + k * rank, rank)
        downs.append(pltpu.make_async_copy(kd_hbm.at[tenant], down.at[at], sems.at[1, k]))
        downs.append(pltpu.make_async_copy(vd_hbm.at[tenant], down.at[after], sems.at[2, k]))
    for copy in downs[1:]:
        copy.start()
    masks = segment_masks(len_ref, (rank, rows), segments)
    slot_of = jnp.zeros((rank, rows), f32)
    for k in range(segments):
        slot = slot_ref[tenant_ref[0, k]].astype(f32)
        slot_of = jnp.where(masks[k], slot, slot_of)
    out_ref[4 * rank :, :] = slot_of.astype(bf16)

    def fold(take):
        total = jnp.zeros((rank, rows), f32)
        for k in range(segments):
            total = jnp.where(masks[k], take(k), total)
        return total.astype(bf16)

    def by_tenant(k):
        return products[pl.ds(pl.multiple_of(tenant_ref[0, k] * rank, rank), rank), :]

    for copy in grads + weights:
        copy.wait()
    if frozen:
        term_ref[...] = frozen_part(gk[...], gv[...], wk[...], wv[...]).astype(term_ref.dtype)
    for copy in ups:
        copy.wait()
    for at, up, grad in ((2, key_up, gk), (3, value_up, gv)):
        products[...] = dot_nt(up[...].reshape(products.shape[0], up.shape[2]), grad[...])
        out_ref[at * rank : (at + 1) * rank, :] = fold(by_tenant)
    for copy in downs:
        copy.wait()
    both = dot_nt(down[...], tok[...])
    for at in (0, 1):
        out_ref[at * rank : (at + 1) * rank, :] = fold(
            lambda k: both[at * half + k * rank : at * half + (k + 1) * rank]
        )


def first_products(frozen, tokens, gk, gv, kd, vd, ku, vu, wk, wv, lengths, tenants, slots):
    rows, width = tokens.shape
    feats = gk.shape[1]
    segments = tenants.shape[1]
    rank = kd.shape[1]
    both = 2 * segments * rank
    hbm = pl.BlockSpec(memory_space=pltpu.HBM)
    vmem = pl.BlockSpec(memory_space=pltpu.VMEM)
    term = (rows, width) if frozen else (16, 128)
    return pl.pallas_call(
        functools.partial(first_kernel, frozen),
        in_specs=[hbm] * 12,
        out_specs=[vmem, vmem],
        out_shape=[
            jax.ShapeDtypeStruct((5 * rank, rows), bf16),
            jax.ShapeDtypeStruct(term, bf16),
        ],
        scratch_shapes=[
            pltpu.SMEM(lengths.shape, jnp.int32),
            pltpu.SMEM(tenants.shape, jnp.int32),
            pltpu.SMEM(slots.shape, jnp.int32),
            pltpu.VMEM((rows, width), bf16),
            pltpu.VMEM((rows, feats), bf16),
            pltpu.VMEM((rows, feats), bf16),
            pltpu.VMEM((both, width), bf16),
            pltpu.VMEM(ku.shape, bf16),
            pltpu.VMEM(vu.shape, bf16),
            pltpu.VMEM((width, feats), bf16),
            pltpu.VMEM((width, feats), bf16),
            pltpu.VMEM((ku.shape[0] * rank, rows), f32),
            pltpu.SemaphoreType.DMA((4, max(segments, 8))),
        ],
        compiler_params=params(),
        cost_estimate=COST,
        name="first_products",
    )(lengths, tenants, slots, tokens, gk, gv, kd, vd, ku, vu, wk, wv)


def adapter_kernel(
    len_ref, tenant_ref, sums_ref, term_ref, kd_hbm, vd_hbm, out_ref, down, back, sems
):
    segments = tenant_ref.shape[1]
    rank = kd_hbm.shape[1]
    rows = out_ref.shape[0]
    half = segments * rank
    copies = []
    for k in range(segments):
        tenant = tenant_ref[0, k]
        at = pl.ds(k * rank, rank)
        after = pl.ds(half + k * rank, rank)
        copies.append(pltpu.make_async_copy(kd_hbm.at[tenant], down.at[at], sems.at[0, k]))
        copies.append(pltpu.make_async_copy(vd_hbm.at[tenant], down.at[after], sems.at[1, k]))
    for copy in copies:
        copy.start()
    masks = segment_masks(len_ref, (rank, rows), segments)
    for at in (0, 1):
        values = ADAPTER_SCALE * sums_ref[(2 + at) * rank : (3 + at) * rank, :].astype(f32)
        for k in range(segments):
            start = at * half + k * rank
            back[start : start + rank, :] = jnp.where(masks[k], values, 0.0).astype(bf16)
    for copy in copies:
        copy.wait()
    out_ref[...] = term_ref[...] + dot_tn(back[...], down[...])


def add_adapters(term, sums, kd, vd, lengths, tenants):
    rows, width = term.shape
    segments = tenants.shape[1]
    rank = kd.shape[1]
    both = 2 * segments * rank
    smem = pl.BlockSpec(memory_space=pltpu.SMEM)
    vmem = pl.BlockSpec(memory_space=pltpu.VMEM)
    hbm = pl.BlockSpec(memory_space=pltpu.HBM)
    return pl.pallas_call(
        adapter_kernel,
        in_specs=[smem, smem, vmem, vmem, hbm, hbm],
        out_specs=vmem,
        out_shape=jax.ShapeDtypeStruct((rows, width), f32),
        scratch_shapes=[
            pltpu.VMEM((both, width), bf16),
            pltpu.VMEM((both, rows), bf16),
            pltpu.SemaphoreType.DMA((2, segments)),
        ],
        compiler_params=params(),
        cost_estimate=COST,
        name="add_adapters",
    )(lengths, tenants, sums, term, kd, vd)


def grads_kernel(count, rank, per_owner, first_ref, *refs):
    sums = refs[:count]
    chunks = refs[count : 2 * count]
    ends = refs[2 * count : 3 * count]
    ka_ref, va_ref, kb_ref, vb_ref, spread_ref = refs[3 * count :]
    size = per_owner * rank
    scale = ADAPTER_SCALE * LOSS_UNSCALE

    @pl.when(pl.program_id(0) == 0)
    def _():
        feats = kb_ref.shape[2]
        rows = sums[0].shape[1]
        wanted = lax.broadcasted_iota(jnp.int32, (size, rows), 0) // rank + first_ref[0]
        b_key = jnp.zeros((size, feats), f32)
        b_value = jnp.zeros((size, feats), f32)
        for n in range(count):
            slot = sums[n][4 * rank : 4 * rank + 1, :].astype(f32).astype(jnp.int32)
            mask = wanted == slot

            def spread(index):
                values = sums[n][index * rank : (index + 1) * rank, :].astype(f32)
                tiled = jnp.concatenate([values] * per_owner, axis=0)
                return jnp.where(mask, tiled, 0.0).astype(bf16)

            columns = slice(n * rows, (n + 1) * rows)
            spread_ref[0:size, columns] = spread(2)
            spread_ref[size:, columns] = spread(3)
            b_key += dot_nn(spread(0), ends[n][:, :feats])
            b_value += dot_nn(spread(1), ends[n][:, feats:])
        kb_ref[...] = (scale * b_key).reshape(kb_ref.shape)
        vb_ref[...] = (scale * b_value).reshape(vb_ref.shape)

    tokens = jnp.concatenate([chunk[...] for chunk in chunks], axis=0)
    product = scale * dot_nn(spread_ref[...], tokens)
    ka_ref[...] = product[:size].reshape(ka_ref.shape)
    va_ref[...] = product[size:].reshape(va_ref.shape)


def adapter_grads(first, sums, sent, rank, per_owner, width, feats):
    count = len(sums)
    rows = sent[0].shape[0]
    chunk = 2 * feats
    steps = width // chunk
    a_spec = pl.BlockSpec((per_owner, rank, chunk), lambda i: (0, 0, i))
    b_spec = pl.BlockSpec((per_owner, rank, feats), lambda i: (0, 0, 0))
    return pl.pallas_call(
        functools.partial(grads_kernel, count, rank, per_owner),
        grid=(steps,),
        in_specs=[pl.BlockSpec(memory_space=pltpu.SMEM)]
        + [pl.BlockSpec(sums[0].shape, lambda i: (0, 0))] * count
        + [pl.BlockSpec((rows, chunk), lambda i: (0, i))] * count
        + [pl.BlockSpec((rows, chunk), lambda i: (0, steps))] * count,
        out_specs=[a_spec, a_spec, b_spec, b_spec],
        out_shape=[
            jax.ShapeDtypeStruct((per_owner, rank, width), f32),
            jax.ShapeDtypeStruct((per_owner, rank, width), f32),
            jax.ShapeDtypeStruct((per_owner, rank, feats), f32),
            jax.ShapeDtypeStruct((per_owner, rank, feats), f32),
        ],
        scratch_shapes=[pltpu.VMEM((2 * per_owner * rank, count * rows), bf16)],
        compiler_params=params(),
        cost_estimate=COST,
        name="adapter_grads",
    )(first, *sums, *sent, *sent)


def swap(values, axis, bit, size):
    return lax.ppermute(values, axis, [(i, i ^ bit) for i in range(size)])


def local(
    tokens, gk, gv, wk, wv, kd, vd, ku, vu, segment_length, segment_tenant, adapter_output_slot
):
    rows, width = tokens.shape
    feats = gk.shape[1]
    adapters, rank, _ = kd.shape
    n_tensor = lax.axis_size("tensor")
    n_dp = lax.axis_size("dp")
    per_owner = adapters // n_dp
    first = (lax.axis_index("dp") * per_owner).astype(jnp.int32).reshape(1)
    in_hbm = functools.partial(pltpu.with_memory_space_constraint, memory_space=pltpu.HBM)
    kd, vd = in_hbm(kd), in_hbm(vd)
    large = [in_hbm(array) for array in (gk, gv, wk, wv)]
    halving = n_tensor == 4

    part, x0 = first_products(
        halving, in_hbm(tokens), large[0], large[1], kd, vd, in_hbm(ku), in_hbm(vu), *large[2:],
        in_hbm(segment_length), in_hbm(segment_tenant), in_hbm(adapter_output_slot),
    )
    products, slot_rows = part[: 4 * rank], part[4 * rank :]
    if halving:
        r1 = swap(x0, "tensor", 1, 4)
        others = [swap(products, "tensor", bit, 4) for bit in (1, 2, 3)]
        tokens, wk, x0 = lax.optimization_barrier((tokens, wk, x0))
        sent = jnp.concatenate([tokens, gk, gv], axis=1)
        x2, x1, own = frozen_blocks(large[0], large[1], in_hbm(wk), large[3], width, (f32, bf16, f32))
        x2, x1, r1, *others = lax.optimization_barrier((x2, x1, r1, *others))
        x2 = (x2 + r1.astype(f32)).astype(bf16)
        r3 = swap(x2, "tensor", 2, 4)
        total = products.astype(f32)
        for other in others:
            total = total + other.astype(f32)
    else:
        sent = jnp.concatenate([tokens, gk, gv], axis=1)
        total = lax.psum(products.astype(f32), "tensor")
        term = dot_nt(gk, wk) + dot_nt(gv, wv)
        own = lax.psum_scatter(
            term.astype(bf16), "tensor", scatter_dimension=1, tiled=True
        ).astype(f32)
    sums = jnp.concatenate([total.astype(bf16), slot_rows], axis=0)
    if halving:
        x1, sums = lax.optimization_barrier((x1, sums))
        r4 = swap(x1, "tensor", 1, 4)

    if n_dp == 4:
        sent_across, sent_core = swap(sent, "dp", 2, 4), swap(sent, "dp", 1, 4)
        pair = jnp.concatenate([sums, swap(sums, "dp", 1, 4)], axis=0)
        pairs = [pair, swap(pair, "dp", 2, 4)]
        all_sums = [half[n * sums.shape[0] : (n + 1) * sums.shape[0]] for half in pairs for n in (0, 1)]
        all_sent = [sent, sent_core, sent_across, swap(sent_across, "dp", 1, 4)]
    else:
        gathered = lax.all_gather(sent, "dp")
        all_sent = [gathered[i] for i in range(n_dp)]
        gathered = lax.all_gather(sums, "dp")
        all_sums = [gathered[i] for i in range(n_dp)]

    own = add_adapters(own, sums, kd, vd, segment_length, segment_tenant)
    grads = adapter_grads(first, all_sums, all_sent, rank, per_owner, width, feats)
    if halving:
        own, *grads = lax.optimization_barrier((own, *grads))
        own = own + r3.astype(f32) + r4.astype(f32)
    input_gradient = own.astype(bf16)
    return (input_gradient, *grads)


def solution(mesh):
    placed = (
        P(("group", "dp"), "tensor"),
        P(("group", "dp"), "tensor"),
        P(("group", "dp"), "tensor"),
        P(None, "tensor"),
        P(None, "tensor"),
        P(None, None, "tensor"),
        P(None, None, "tensor"),
        P(None, None, "tensor"),
        P(None, None, "tensor"),
        P(("group", "dp"), None),
        P(("group", "dp"), None),
        P("group"),
    )
    return jax.shard_map(
        local,
        mesh=mesh,
        in_specs=placed,
        out_specs=(
            P(("group", "dp"), "tensor"),
            P(("group", "dp"), None, "tensor"),
            P(("group", "dp"), None, "tensor"),
            P(("group", "dp"), None, "tensor"),
            P(("group", "dp"), None, "tensor"),
        ),
        check_vma=False,
    )
```

```python
import functools

import jax
import jax.numpy as jnp
from jax import lax
from jax.experimental import pallas as pl
from jax.experimental.pallas import tpu as pltpu
from jax.sharding import PartitionSpec as P

ADAPTER_SCALE = 2.0
LOSS_UNSCALE = 0.125
VMEM_BYTES = 20 * 1024 * 1024
COST = pl.CostEstimate(flops=0, bytes_accessed=0, transcendentals=0)

f32 = jnp.float32
bf16 = jnp.bfloat16


def dot_nt(former, latter):
    return lax.dot_general(former, latter, (((1,), (1,)), ((), ())), preferred_element_type=f32)


def dot_nn(former, latter):
    return lax.dot_general(former, latter, (((1,), (0,)), ((), ())), preferred_element_type=f32)


def dot_tn(former, latter):
    return lax.dot_general(former, latter, (((0,), (0,)), ((), ())), preferred_element_type=f32)


def params():
    return pltpu.CompilerParams(vmem_limit_bytes=VMEM_BYTES)


def frozen_part(gk, gv, wk, wv):
    return dot_nt(gk, wk) + dot_nt(gv, wv)


def frozen_copies(block, width, wk_hbm, wv_hbm, wk, wv, sems):
    rows = pl.ds(pl.multiple_of(block * width, width), width)
    return [
        pltpu.make_async_copy(wk_hbm.at[rows], wk, sems.at[0]),
        pltpu.make_async_copy(wv_hbm.at[rows], wv, sems.at[1]),
    ]


def frozen_kernel(
    first_ref, gk_hbm, gv_hbm, wk_hbm, wv_hbm, x2a_ref, x2b_ref, x1_ref, own_ref,
    gk, gv, wk, wv, sems,
):
    rows, width = x1_ref.shape
    z = lax.axis_index("tensor")
    head = [
        pltpu.make_async_copy(gk_hbm, gk, sems.at[3, 0]),
        pltpu.make_async_copy(gv_hbm, gv, sems.at[3, 1]),
    ]
    body = [
        frozen_copies(block, width, wk_hbm, wv_hbm, wk.at[n], wv.at[n], sems.at[n])
        for n, block in enumerate((z ^ 2, z ^ 1, z))
    ]
    for copies in (head, *body):
        for copy in copies:
            copy.start()
    ahead = x2a_ref.shape[1] - rows
    x2a_ref[:, ahead:] = first_ref[:, ahead:].astype(f32)
    for copy in head + body[0]:
        copy.wait()
    x2a_ref[:, :ahead] = frozen_part(gk[...], gv[...], wk[0, :ahead], wv[0, :ahead])
    x2b_ref[...] = frozen_part(gk[...], gv[...], wk[0, ahead:], wv[0, ahead:])
    for n, out in ((1, x1_ref), (2, own_ref)):
        for copy in body[n]:
            copy.wait()
        out[...] = frozen_part(gk[...], gv[...], wk[n], wv[n]).astype(out.dtype)


def frozen_blocks(first_part, gk, gv, wk, wv, width):
    rows, feats = gk.shape
    hbm = pl.BlockSpec(memory_space=pltpu.HBM)
    vmem = pl.BlockSpec(memory_space=pltpu.VMEM)
    return pl.pallas_call(
        frozen_kernel,
        in_specs=[vmem] + [hbm] * 4,
        out_specs=[vmem] * 4,
        out_shape=[
            jax.ShapeDtypeStruct(first_part.shape, f32),
            jax.ShapeDtypeStruct((rows, width + rows - first_part.shape[1]), f32),
            jax.ShapeDtypeStruct((rows, width), bf16),
            jax.ShapeDtypeStruct((rows, width), f32),
        ],
        scratch_shapes=[
            pltpu.VMEM((rows, feats), bf16),
            pltpu.VMEM((rows, feats), bf16),
            pltpu.VMEM((3, width, feats), bf16),
            pltpu.VMEM((3, width, feats), bf16),
            pltpu.SemaphoreType.DMA((4, 2)),
        ],
        compiler_params=params(),
        cost_estimate=COST,
        name="frozen_blocks",
    )(first_part, gk, gv, wk, wv)


def finish_kernel(own_ref, x1_ref, x2b_ref, out_ref):
    ahead = own_ref.shape[1] - x2b_ref.shape[1]
    total = own_ref[...] + x1_ref[...].astype(f32)
    out_ref[:, :ahead] = total[:, :ahead].astype(bf16)
    out_ref[:, ahead:] = (total[:, ahead:] + x2b_ref[...].astype(f32)).astype(bf16)


def finish(own, x1, x2b):
    vmem = pl.BlockSpec(memory_space=pltpu.VMEM)
    return pl.pallas_call(
        finish_kernel,
        in_specs=[vmem] * 3,
        out_specs=vmem,
        out_shape=jax.ShapeDtypeStruct(own.shape, bf16),
        compiler_params=params(),
        cost_estimate=COST,
        name="finish",
    )(own, x1, x2b)


def segment_masks(len_ref, shape, segments):
    position = lax.broadcasted_iota(jnp.int32, shape, 1)
    masks = []
    total = jnp.int32(0)
    for k in range(segments):
        begin = total
        total = total + len_ref[0, k]
        masks.append((position >= begin) & (position < total))
    return masks


def first_kernel(
    frozen, len_hbm, tenant_hbm, slot_hbm, tok_hbm, gk_hbm, gv_hbm, kd_hbm, vd_hbm, ku_hbm, vu_hbm,
    wk_hbm, wv_hbm, out_ref, slots_ref, *refs,
):
    if frozen:
        last_ref, *refs = refs
    (
        len_ref, tenant_ref, slot_ref, tok, gk, gv, down, key_up, value_up, wk, wv, products, sems,
    ) = refs
    segments = tenant_ref.shape[1]
    rank = kd_hbm.shape[1]
    rows, width = tok.shape
    half = segments * rank
    scalars = [
        pltpu.make_async_copy(tenant_hbm, tenant_ref, sems.at[0, 0]),
        pltpu.make_async_copy(len_hbm, len_ref, sems.at[0, 1]),
        pltpu.make_async_copy(slot_hbm, slot_ref, sems.at[0, 2]),
    ]
    grads = [
        pltpu.make_async_copy(gk_hbm, gk, sems.at[0, 3]),
        pltpu.make_async_copy(gv_hbm, gv, sems.at[0, 4]),
    ]
    weights = []
    if frozen:
        weights = frozen_copies(
            lax.axis_index("tensor") ^ 3, width, wk_hbm, wv_hbm, wk, wv, sems.at[3]
        )
    ups = [
        pltpu.make_async_copy(ku_hbm, key_up, sems.at[0, 5]),
        pltpu.make_async_copy(vu_hbm, value_up, sems.at[0, 6]),
    ]
    downs = [pltpu.make_async_copy(tok_hbm, tok, sems.at[0, 7])]
    for copy in scalars + grads + weights + ups + downs:
        copy.start()
    for copy in scalars:
        copy.wait()
    for k in range(segments):
        tenant = tenant_ref[0, k]
        at = pl.ds(k * rank, rank)
        after = pl.ds(half + k * rank, rank)
        downs.append(pltpu.make_async_copy(kd_hbm.at[tenant], down.at[at], sems.at[1, k]))
        downs.append(pltpu.make_async_copy(vd_hbm.at[tenant], down.at[after], sems.at[2, k]))
    for copy in downs[1:]:
        copy.start()
    masks = segment_masks(len_ref, (rank, rows), segments)
    slot_of = jnp.zeros((rank, rows), f32)
    for k in range(segments):
        slot = slot_ref[tenant_ref[0, k]].astype(f32)
        slot_of = jnp.where(masks[k], slot, slot_of)
    slots_ref[...] = slot_of.astype(bf16)
    ahead = out_ref.shape[1] - rows
    if frozen:
        out_ref[4 * rank :, ahead:] = jnp.zeros((rows - 4 * rank, rows), bf16)

    def put(at, values):
        out_ref[at * rank : (at + 1) * rank, ahead:] = values

    def fold(take):
        total = jnp.zeros((rank, rows), f32)
        for k in range(segments):
            total = jnp.where(masks[k], take(k), total)
        return total.astype(bf16)

    def by_tenant(k):
        return products[pl.ds(pl.multiple_of(tenant_ref[0, k] * rank, rank), rank), :]

    for copy in grads + weights:
        copy.wait()
    if frozen:
        out_ref[:, :ahead] = frozen_part(gk[...], gv[...], wk[:ahead], wv[:ahead]).astype(bf16)
        last_ref[...] = frozen_part(gk[...], gv[...], wk[ahead:], wv[ahead:]).astype(bf16)
    for copy in ups:
        copy.wait()
    for at, up, grad in ((2, key_up, gk), (3, value_up, gv)):
        products[...] = dot_nt(up[...].reshape(products.shape[0], up.shape[2]), grad[...])
        put(at, fold(by_tenant))
    for copy in downs:
        copy.wait()
    both = dot_nt(down[...], tok[...])
    for at in (0, 1):
        put(at, fold(lambda k: both[at * half + k * rank : at * half + (k + 1) * rank]))


def first_products(frozen, tokens, gk, gv, kd, vd, ku, vu, wk, wv, lengths, tenants, slots):
    rows, width = tokens.shape
    feats = gk.shape[1]
    segments = tenants.shape[1]
    rank = kd.shape[1]
    both = 2 * segments * rank
    hbm = pl.BlockSpec(memory_space=pltpu.HBM)
    vmem = pl.BlockSpec(memory_space=pltpu.VMEM)
    shapes = [(4 * rank, rows), (rank, rows)]
    if frozen:
        ahead = width * 5 // 16
        shapes = [(rows, ahead + rows), (rank, rows), (rows, width - ahead)]
    return pl.pallas_call(
        functools.partial(first_kernel, frozen),
        in_specs=[hbm] * 12,
        out_specs=[vmem] * len(shapes),
        out_shape=[jax.ShapeDtypeStruct(shape, bf16) for shape in shapes],
        scratch_shapes=[
            pltpu.SMEM(lengths.shape, jnp.int32),
            pltpu.SMEM(tenants.shape, jnp.int32),
            pltpu.SMEM(slots.shape, jnp.int32),
            pltpu.VMEM((rows, width), bf16),
            pltpu.VMEM((rows, feats), bf16),
            pltpu.VMEM((rows, feats), bf16),
            pltpu.VMEM((both, width), bf16),
            pltpu.VMEM(ku.shape, bf16),
            pltpu.VMEM(vu.shape, bf16),
            pltpu.VMEM((width, feats), bf16),
            pltpu.VMEM((width, feats), bf16),
            pltpu.VMEM((ku.shape[0] * rank, rows), f32),
            pltpu.SemaphoreType.DMA((4, max(segments, 8))),
        ],
        compiler_params=params(),
        cost_estimate=COST,
        name="first_products",
    )(lengths, tenants, slots, tokens, gk, gv, kd, vd, ku, vu, wk, wv)


def adapter_kernel(
    frozen, len_ref, tenant_ref, sums_ref, term_ref, *refs
):
    if frozen:
        ahead_ref, *refs = refs
    kd_hbm, vd_hbm, out_ref, down, back, sems = refs
    segments = tenant_ref.shape[1]
    rank = kd_hbm.shape[1]
    rows = out_ref.shape[0]
    half = segments * rank
    copies = []
    for k in range(segments):
        tenant = tenant_ref[0, k]
        at = pl.ds(k * rank, rank)
        after = pl.ds(half + k * rank, rank)
        copies.append(pltpu.make_async_copy(kd_hbm.at[tenant], down.at[at], sems.at[0, k]))
        copies.append(pltpu.make_async_copy(vd_hbm.at[tenant], down.at[after], sems.at[1, k]))
    for copy in copies:
        copy.start()
    masks = segment_masks(len_ref, (rank, rows), segments)
    for at in (0, 1):
        values = ADAPTER_SCALE * sums_ref[(2 + at) * rank : (3 + at) * rank, :].astype(f32)
        for k in range(segments):
            start = at * half + k * rank
            back[start : start + rank, :] = jnp.where(masks[k], values, 0.0).astype(bf16)
    for copy in copies:
        copy.wait()
    total = term_ref[...] + dot_tn(back[...], down[...])
    out_ref[...] = total
    if frozen:
        ahead = ahead_ref.shape[1] - rows
        out_ref[:, :ahead] = total[:, :ahead] + ahead_ref[:, :ahead].astype(f32)


def add_adapters(terms, sums, kd, vd, lengths, tenants):
    rows, width = terms[0].shape
    segments = tenants.shape[1]
    rank = kd.shape[1]
    both = 2 * segments * rank
    smem = pl.BlockSpec(memory_space=pltpu.SMEM)
    vmem = pl.BlockSpec(memory_space=pltpu.VMEM)
    hbm = pl.BlockSpec(memory_space=pltpu.HBM)
    return pl.pallas_call(
        functools.partial(adapter_kernel, len(terms) > 1),
        in_specs=[smem, smem, vmem] + [vmem] * len(terms) + [hbm, hbm],
        out_specs=vmem,
        out_shape=jax.ShapeDtypeStruct((rows, width), f32),
        scratch_shapes=[
            pltpu.VMEM((both, width), bf16),
            pltpu.VMEM((both, rows), bf16),
            pltpu.SemaphoreType.DMA((2, segments)),
        ],
        compiler_params=params(),
        cost_estimate=COST,
        name="add_adapters",
    )(lengths, tenants, sums, *terms, kd, vd)


def grads_kernel(count, rank, per_owner, first_ref, *refs):
    sums = refs[:count]
    chunks = refs[count : 2 * count]
    ends = refs[2 * count : 3 * count]
    ka_ref, va_ref, kb_ref, vb_ref, spread_ref = refs[3 * count :]
    size = per_owner * rank
    scale = ADAPTER_SCALE * LOSS_UNSCALE

    @pl.when(pl.program_id(0) == 0)
    def _():
        feats = kb_ref.shape[2]
        rows = sums[0].shape[1]
        wanted = lax.broadcasted_iota(jnp.int32, (size, rows), 0) // rank + first_ref[0]
        b_key = jnp.zeros((size, feats), f32)
        b_value = jnp.zeros((size, feats), f32)
        for n in range(count):
            slot = sums[n][4 * rank : 4 * rank + 1, :].astype(f32).astype(jnp.int32)
            mask = wanted == slot

            def spread(index):
                values = sums[n][index * rank : (index + 1) * rank, :].astype(f32)
                tiled = jnp.concatenate([values] * per_owner, axis=0)
                return jnp.where(mask, tiled, 0.0).astype(bf16)

            columns = slice(n * rows, (n + 1) * rows)
            spread_ref[0:size, columns] = spread(2)
            spread_ref[size:, columns] = spread(3)
            b_key += dot_nn(spread(0), ends[n][:, :feats])
            b_value += dot_nn(spread(1), ends[n][:, feats:])
        kb_ref[...] = (scale * b_key).reshape(kb_ref.shape)
        vb_ref[...] = (scale * b_value).reshape(vb_ref.shape)

    tokens = jnp.concatenate([chunk[...] for chunk in chunks], axis=0)
    product = scale * dot_nn(spread_ref[...], tokens)
    ka_ref[...] = product[:size].reshape(ka_ref.shape)
    va_ref[...] = product[size:].reshape(va_ref.shape)


def adapter_grads(first, sums, sent, rank, per_owner, width, feats):
    count = len(sums)
    rows = sent[0].shape[0]
    chunk = 2 * feats
    steps = width // chunk
    a_spec = pl.BlockSpec((per_owner, rank, chunk), lambda i: (0, 0, i))
    b_spec = pl.BlockSpec((per_owner, rank, feats), lambda i: (0, 0, 0))
    return pl.pallas_call(
        functools.partial(grads_kernel, count, rank, per_owner),
        grid=(steps,),
        in_specs=[pl.BlockSpec(memory_space=pltpu.SMEM)]
        + [pl.BlockSpec(sums[0].shape, lambda i: (0, 0))] * count
        + [pl.BlockSpec((rows, chunk), lambda i: (0, i))] * count
        + [pl.BlockSpec((rows, chunk), lambda i: (0, steps))] * count,
        out_specs=[a_spec, a_spec, b_spec, b_spec],
        out_shape=[
            jax.ShapeDtypeStruct((per_owner, rank, width), f32),
            jax.ShapeDtypeStruct((per_owner, rank, width), f32),
            jax.ShapeDtypeStruct((per_owner, rank, feats), f32),
            jax.ShapeDtypeStruct((per_owner, rank, feats), f32),
        ],
        scratch_shapes=[pltpu.VMEM((2 * per_owner * rank, count * rows), bf16)],
        compiler_params=params(),
        cost_estimate=COST,
        name="adapter_grads",
    )(first, *sums, *sent, *sent)


def swap(values, axis, bit, size):
    return lax.ppermute(values, axis, [(i, i ^ bit) for i in range(size)])


def local(
    tokens, gk, gv, wk, wv, kd, vd, ku, vu, segment_length, segment_tenant, adapter_output_slot
):
    rows, width = tokens.shape
    feats = gk.shape[1]
    adapters, rank, _ = kd.shape
    n_tensor = lax.axis_size("tensor")
    n_dp = lax.axis_size("dp")
    per_owner = adapters // n_dp
    first = (lax.axis_index("dp") * per_owner).astype(jnp.int32).reshape(1)
    in_hbm = functools.partial(pltpu.with_memory_space_constraint, memory_space=pltpu.HBM)
    kd, vd = in_hbm(kd), in_hbm(vd)
    large = [in_hbm(array) for array in (gk, gv, wk, wv)]
    halving = n_tensor == 4

    first_part, slot_rows, *second = first_products(
        halving, in_hbm(tokens), large[0], large[1], kd, vd, in_hbm(ku), in_hbm(vu), *large[2:],
        in_hbm(segment_length), in_hbm(segment_tenant), in_hbm(adapter_output_slot),
    )
    tokens, first_part, *second = lax.optimization_barrier((tokens, first_part, *second))
    sent = jnp.concatenate([tokens, gk, gv], axis=1)
    if halving:
        ahead = first_part.shape[1] - rows
        r1a = swap(first_part, "tensor", 1, 4)
        r1b = swap(second[0], "tensor", 1, 4)
        x2a, x2b, x1, own = frozen_blocks(first_part, *large, width)
        x2a, r1a = lax.optimization_barrier((x2a, r1a))
        x2a = (x2a + r1a.astype(f32)).astype(bf16)
        r3a = swap(x2a, "tensor", 2, 4)
        x2b, x1, r1b = lax.optimization_barrier((x2b, x1, r1b))
        x2b = (x2b + r1b.astype(f32)).astype(bf16)
        r3b = swap(x2b, "tensor", 2, 4)
        r4 = swap(x1, "tensor", 1, 4)
        x2b, r3a, x2a = lax.optimization_barrier((x2b, r3a, x2a))
        total = x2a[: 4 * rank, ahead:].astype(f32) + r3a[: 4 * rank, ahead:].astype(f32)
        terms = [own, r3a]
    else:
        total = lax.psum(first_part.astype(f32), "tensor")
        term = dot_nt(gk, wk) + dot_nt(gv, wv)
        terms = [
            lax.psum_scatter(
                term.astype(bf16), "tensor", scatter_dimension=1, tiled=True
            ).astype(f32)
        ]
    sums = jnp.concatenate([total.astype(bf16), slot_rows], axis=0)

    if n_dp == 4:
        sent_across, sent_core = swap(sent, "dp", 2, 4), swap(sent, "dp", 1, 4)
        pair = jnp.concatenate([sums, swap(sums, "dp", 1, 4)], axis=0)
        pairs = [pair, swap(pair, "dp", 2, 4)]
        size = sums.shape[0]
        all_sums = [two[n * size : (n + 1) * size] for two in pairs for n in (0, 1)]
        all_sent = [sent, sent_core, sent_across, swap(sent_across, "dp", 1, 4)]
    else:
        gathered = lax.all_gather(sent, "dp")
        all_sent = [gathered[i] for i in range(n_dp)]
        gathered = lax.all_gather(sums, "dp")
        all_sums = [gathered[i] for i in range(n_dp)]

    own = add_adapters(terms, sums, kd, vd, segment_length, segment_tenant)
    grads = adapter_grads(first, all_sums, all_sent, rank, per_owner, width, feats)
    if halving:
        own, *grads = lax.optimization_barrier((own, *grads))
        input_gradient = finish(own, r4, r3b)
    else:
        input_gradient = own.astype(bf16)
    return (input_gradient, *grads)


def solution(mesh):
    placed = (
        P(("group", "dp"), "tensor"),
        P(("group", "dp"), "tensor"),
        P(("group", "dp"), "tensor"),
        P(None, "tensor"),
        P(None, "tensor"),
        P(None, None, "tensor"),
        P(None, None, "tensor"),
        P(None, None, "tensor"),
        P(None, None, "tensor"),
        P(("group", "dp"), None),
        P(("group", "dp"), None),
        P("group"),
    )
    return jax.shard_map(
        local,
        mesh=mesh,
        in_specs=placed,
        out_specs=(
            P(("group", "dp"), "tensor"),
            P(("group", "dp"), None, "tensor"),
            P(("group", "dp"), None, "tensor"),
            P(("group", "dp"), None, "tensor"),
            P(("group", "dp"), None, "tensor"),
        ),
        check_vma=False,
    )
```

```python
import functools

import jax
import jax.numpy as jnp
from jax import lax
from jax.experimental import pallas as pl
from jax.experimental.pallas import tpu as pltpu
from jax.sharding import PartitionSpec as P

ADAPTER_SCALE = 2.0
LOSS_UNSCALE = 0.125
VMEM_BYTES = 16 * 1024 * 1024
COST = pl.CostEstimate(flops=0, bytes_accessed=0, transcendentals=0)

f32 = jnp.float32
bf16 = jnp.bfloat16


def dot_nt(former, latter):
    return lax.dot_general(former, latter, (((1,), (1,)), ((), ())), preferred_element_type=f32)


def dot_nn(former, latter):
    return lax.dot_general(former, latter, (((1,), (0,)), ((), ())), preferred_element_type=f32)


def dot_tn(former, latter):
    return lax.dot_general(former, latter, (((0,), (0,)), ((), ())), preferred_element_type=f32)


def params():
    return pltpu.CompilerParams(vmem_limit_bytes=VMEM_BYTES)


def frozen_part(gk, gv, wk, wv):
    return dot_nt(gk, wk) + dot_nt(gv, wv)


def frozen_copies(first, count, wk_hbm, wv_hbm, wk, wv, key_sem, value_sem):
    rows = pl.ds(pl.multiple_of(first, 128), count)
    return [
        pltpu.make_async_copy(wk_hbm.at[rows], wk, key_sem),
        pltpu.make_async_copy(wv_hbm.at[rows], wv, value_sem),
    ]


def frozen_kernel(
    first_ref, gk_hbm, gv_hbm, wk_hbm, wv_hbm, x0b_ref, x2a_ref, x2b_ref, x1_ref, gk, gv, wk, wv,
    sems,
):
    rows, width = x1_ref.shape
    tail = x0b_ref.shape[1]
    z = lax.axis_index("tensor")
    head = [
        pltpu.make_async_copy(gk_hbm, gk, sems.at[3, 0]),
        pltpu.make_async_copy(gv_hbm, gv, sems.at[3, 1]),
    ]
    body = []
    first = 0
    for n, (start, count) in enumerate(
        (((z ^ 3) * width + width - tail, tail), ((z ^ 2) * width, width), ((z ^ 1) * width, width))
    ):
        at = slice(first, first + count)
        body.append(
            frozen_copies(
                start, count, wk_hbm, wv_hbm, wk.at[at], wv.at[at], sems.at[n, 0], sems.at[n, 1]
            )
        )
        first += count
    for copies in (head, *body):
        for copy in copies:
            copy.start()
    early = x2a_ref.shape[1] - rows
    x2a_ref[:, early:] = first_ref[:, first_ref.shape[1] - rows :].astype(f32)
    for copy in head:
        copy.wait()

    def term(first, count):
        at = slice(first, first + count)
        return frozen_part(gk[...], gv[...], wk[at], wv[at])

    for copy in body[0]:
        copy.wait()
    x0b_ref[...] = term(0, tail).astype(bf16)
    for copy in body[1]:
        copy.wait()
    x2a_ref[:, :early] = term(tail, early)
    x2b_ref[...] = term(tail + early, width - early)
    for copy in body[2]:
        copy.wait()
    x1_ref[...] = term(tail + width, width).astype(bf16)


def frozen_blocks(first_part, gk, gv, wk, wv, width, early):
    rows, feats = gk.shape
    tail = width + rows - first_part.shape[1]
    hbm = pl.BlockSpec(memory_space=pltpu.HBM)
    vmem = pl.BlockSpec(memory_space=pltpu.VMEM)
    return pl.pallas_call(
        frozen_kernel,
        in_specs=[vmem] + [hbm] * 4,
        out_specs=[vmem] * 4,
        out_shape=[
            jax.ShapeDtypeStruct((rows, tail), bf16),
            jax.ShapeDtypeStruct((rows, early + rows), f32),
            jax.ShapeDtypeStruct((rows, width - early), f32),
            jax.ShapeDtypeStruct((rows, width), bf16),
        ],
        scratch_shapes=[
            pltpu.VMEM((rows, feats), bf16),
            pltpu.VMEM((rows, feats), bf16),
            pltpu.VMEM((2 * width + tail, feats), bf16),
            pltpu.VMEM((2 * width + tail, feats), bf16),
            pltpu.SemaphoreType.DMA((4, 2)),
        ],
        compiler_params=params(),
        cost_estimate=COST,
        name="frozen_blocks",
    )(first_part, gk, gv, wk, wv)


def finish_kernel(own_ref, x1_ref, x2b_ref, out_ref):
    ahead = own_ref.shape[1] - x2b_ref.shape[1]
    total = own_ref[...] + x1_ref[...].astype(f32)
    out_ref[:, :ahead] = total[:, :ahead].astype(bf16)
    out_ref[:, ahead:] = (total[:, ahead:] + x2b_ref[...].astype(f32)).astype(bf16)


def finish(own, x1, x2b):
    vmem = pl.BlockSpec(memory_space=pltpu.VMEM)
    return pl.pallas_call(
        finish_kernel,
        in_specs=[vmem] * 3,
        out_specs=vmem,
        out_shape=jax.ShapeDtypeStruct(own.shape, bf16),
        compiler_params=params(),
        cost_estimate=COST,
        name="finish",
    )(own, x1, x2b)


def segment_masks(len_ref, shape, segments):
    position = lax.broadcasted_iota(jnp.int32, shape, 1)
    masks = []
    total = jnp.int32(0)
    for k in range(segments):
        begin = total
        total = total + len_ref[0, k]
        masks.append((position >= begin) & (position < total))
    return masks


def first_kernel(
    frozen, len_hbm, tenant_hbm, slot_hbm, tok_hbm, gk_hbm, gv_hbm, kd_hbm, vd_hbm, ku_hbm, vu_hbm,
    wk_hbm, wv_hbm, out_ref, slots_ref, *refs,
):
    (
        len_ref, tenant_ref, slot_ref, tok, gk, gv, down, key_up, value_up, wk, wv, products, sems,
    ) = refs
    segments = tenant_ref.shape[1]
    rank = kd_hbm.shape[1]
    rows, width = tok.shape
    half = segments * rank
    scalars = [
        pltpu.make_async_copy(tenant_hbm, tenant_ref, sems.at[0, 0]),
        pltpu.make_async_copy(len_hbm, len_ref, sems.at[0, 1]),
        pltpu.make_async_copy(slot_hbm, slot_ref, sems.at[0, 2]),
    ]
    grads = [
        pltpu.make_async_copy(gk_hbm, gk, sems.at[0, 3]),
        pltpu.make_async_copy(gv_hbm, gv, sems.at[0, 4]),
    ]
    weights = []
    if frozen:
        weights = frozen_copies(
            (lax.axis_index("tensor") ^ 3) * width, out_ref.shape[1] - rows, wk_hbm, wv_hbm, wk, wv, sems.at[3, 0],
            sems.at[3, 1],
        )
    ups = [
        pltpu.make_async_copy(ku_hbm, key_up, sems.at[0, 5]),
        pltpu.make_async_copy(vu_hbm, value_up, sems.at[0, 6]),
    ]
    downs = [pltpu.make_async_copy(tok_hbm, tok, sems.at[0, 7])]
    for copy in scalars + grads + weights + ups + downs:
        copy.start()
    for copy in scalars:
        copy.wait()
    for k in range(segments):
        tenant = tenant_ref[0, k]
        at = pl.ds(k * rank, rank)
        after = pl.ds(half + k * rank, rank)
        downs.append(pltpu.make_async_copy(kd_hbm.at[tenant], down.at[at], sems.at[1, k]))
        downs.append(pltpu.make_async_copy(vd_hbm.at[tenant], down.at[after], sems.at[2, k]))
    for copy in downs[1:]:
        copy.start()
    masks = segment_masks(len_ref, (rank, rows), segments)
    slot_of = jnp.zeros((rank, rows), f32)
    for k in range(segments):
        slot = slot_ref[tenant_ref[0, k]].astype(f32)
        slot_of = jnp.where(masks[k], slot, slot_of)
    slots_ref[...] = slot_of.astype(bf16)
    ahead = out_ref.shape[1] - rows
    if frozen:
        out_ref[4 * rank :, ahead:] = jnp.zeros((rows - 4 * rank, rows), bf16)

    def put(at, values):
        out_ref[at * rank : (at + 1) * rank, ahead:] = values

    def fold(take):
        total = jnp.zeros((rank, rows), f32)
        for k in range(segments):
            total = jnp.where(masks[k], take(k), total)
        return total.astype(bf16)

    def by_tenant(k):
        return products[pl.ds(pl.multiple_of(tenant_ref[0, k] * rank, rank), rank), :]

    for copy in grads + weights:
        copy.wait()
    if frozen:
        out_ref[:, :ahead] = frozen_part(gk[...], gv[...], wk[...], wv[...]).astype(bf16)
    for copy in ups:
        copy.wait()
    for at, up, grad in ((2, key_up, gk), (3, value_up, gv)):
        products[...] = dot_nt(up[...].reshape(products.shape[0], up.shape[2]), grad[...])
        put(at, fold(by_tenant))
    for copy in downs:
        copy.wait()
    both = dot_nt(down[...], tok[...])
    for at in (0, 1):
        put(at, fold(lambda k: both[at * half + k * rank : at * half + (k + 1) * rank]))


def first_products(frozen, tokens, gk, gv, kd, vd, ku, vu, wk, wv, lengths, tenants, slots):
    rows, width = tokens.shape
    feats = gk.shape[1]
    segments = tenants.shape[1]
    rank = kd.shape[1]
    both = 2 * segments * rank
    hbm = pl.BlockSpec(memory_space=pltpu.HBM)
    vmem = pl.BlockSpec(memory_space=pltpu.VMEM)
    shapes = [(4 * rank, rows), (rank, rows)]
    weight = pltpu.VMEM((frozen or 16, feats), bf16)
    if frozen:
        shapes = [(rows, frozen + rows), (rank, rows)]
    return pl.pallas_call(
        functools.partial(first_kernel, frozen),
        in_specs=[hbm] * 12,
        out_specs=[vmem] * len(shapes),
        out_shape=[jax.ShapeDtypeStruct(shape, bf16) for shape in shapes],
        scratch_shapes=[
            pltpu.SMEM(lengths.shape, jnp.int32),
            pltpu.SMEM(tenants.shape, jnp.int32),
            pltpu.SMEM(slots.shape, jnp.int32),
            pltpu.VMEM((rows, width), bf16),
            pltpu.VMEM((rows, feats), bf16),
            pltpu.VMEM((rows, feats), bf16),
            pltpu.VMEM((both, width), bf16),
            pltpu.VMEM(ku.shape, bf16),
            pltpu.VMEM(vu.shape, bf16),
            weight,
            weight,
            pltpu.VMEM((ku.shape[0] * rank, rows), f32),
            pltpu.SemaphoreType.DMA((4, max(segments, 8))),
        ],
        compiler_params=params(),
        cost_estimate=COST,
        name="first_products",
    )(lengths, tenants, slots, tokens, gk, gv, kd, vd, ku, vu, wk, wv)


def adapter_kernel(
    frozen, len_ref, tenant_ref, sums_ref, ahead_ref, gk_hbm, gv_hbm, wk_hbm, wv_hbm, kd_hbm,
    vd_hbm, out_ref, gk, gv, wk, wv, down, back, sems,
):
    segments = tenant_ref.shape[1]
    rank = kd_hbm.shape[1]
    rows, width = out_ref.shape
    half = segments * rank
    copies = []
    if frozen:
        copies = [
            pltpu.make_async_copy(gk_hbm, gk, sems.at[2, 2]),
            pltpu.make_async_copy(gv_hbm, gv, sems.at[2, 3]),
        ] + frozen_copies(
            lax.axis_index("tensor") * width, width, wk_hbm, wv_hbm, wk, wv, sems.at[2, 0],
            sems.at[2, 1],
        )
    for k in range(segments):
        tenant = tenant_ref[0, k]
        at = pl.ds(k * rank, rank)
        after = pl.ds(half + k * rank, rank)
        copies.append(pltpu.make_async_copy(kd_hbm.at[tenant], down.at[at], sems.at[0, k]))
        copies.append(pltpu.make_async_copy(vd_hbm.at[tenant], down.at[after], sems.at[1, k]))
    for copy in copies:
        copy.start()
    masks = segment_masks(len_ref, (rank, rows), segments)
    for at in (0, 1):
        values = ADAPTER_SCALE * sums_ref[(2 + at) * rank : (3 + at) * rank, :].astype(f32)
        for k in range(segments):
            start = at * half + k * rank
            back[start : start + rank, :] = jnp.where(masks[k], values, 0.0).astype(bf16)
    for copy in copies:
        copy.wait()
    total = dot_tn(back[...], down[...])
    if frozen:
        total += frozen_part(gk[...], gv[...], wk[...], wv[...])
    ahead = min(width, ahead_ref.shape[1] - rows) if frozen else width
    out_ref[:, :ahead] = total[:, :ahead] + ahead_ref[:, :ahead].astype(f32)
    if ahead < width:
        out_ref[:, ahead:] = total[:, ahead:]


def add_adapters(frozen, ahead_sum, sums, gk, gv, wk, wv, kd, vd, lengths, tenants):
    rows, feats = gk.shape
    width = kd.shape[2]
    segments = tenants.shape[1]
    rank = kd.shape[1]
    both = 2 * segments * rank
    smem = pl.BlockSpec(memory_space=pltpu.SMEM)
    vmem = pl.BlockSpec(memory_space=pltpu.VMEM)
    hbm = pl.BlockSpec(memory_space=pltpu.HBM)
    weight = pltpu.VMEM((width, feats) if frozen else (16, feats), bf16)
    return pl.pallas_call(
        functools.partial(adapter_kernel, frozen),
        in_specs=[smem, smem, vmem, vmem] + [hbm] * 6,
        out_specs=vmem,
        out_shape=jax.ShapeDtypeStruct((rows, width), f32),
        scratch_shapes=[
            pltpu.VMEM((rows, feats), bf16),
            pltpu.VMEM((rows, feats), bf16),
            weight,
            weight,
            pltpu.VMEM((both, width), bf16),
            pltpu.VMEM((both, rows), bf16),
            pltpu.SemaphoreType.DMA((3, max(segments, 8))),
        ],
        compiler_params=params(),
        cost_estimate=COST,
        name="add_adapters",
    )(lengths, tenants, sums, ahead_sum, gk, gv, wk, wv, kd, vd)


def grads_kernel(count, rank, per_owner, first_ref, *refs):
    sums = refs[:count]
    chunks = refs[count : 2 * count]
    ends = refs[2 * count : 3 * count]
    ka_ref, va_ref, kb_ref, vb_ref, spread_ref = refs[3 * count :]
    size = per_owner * rank
    scale = ADAPTER_SCALE * LOSS_UNSCALE

    @pl.when(pl.program_id(0) == 0)
    def _():
        feats = kb_ref.shape[2]
        rows = sums[0].shape[1]
        wanted = lax.broadcasted_iota(jnp.int32, (size, rows), 0) // rank + first_ref[0]
        b_key = jnp.zeros((size, feats), f32)
        b_value = jnp.zeros((size, feats), f32)
        for n in range(count):
            slot = sums[n][4 * rank : 4 * rank + 1, :].astype(f32).astype(jnp.int32)
            mask = wanted == slot

            def spread(index):
                values = sums[n][index * rank : (index + 1) * rank, :].astype(f32)
                tiled = jnp.concatenate([values] * per_owner, axis=0)
                return jnp.where(mask, tiled, 0.0).astype(bf16)

            columns = slice(n * rows, (n + 1) * rows)
            spread_ref[0:size, columns] = spread(2)
            spread_ref[size:, columns] = spread(3)
            b_key += dot_nn(spread(0), ends[n][:, :feats])
            b_value += dot_nn(spread(1), ends[n][:, feats:])
        kb_ref[...] = (scale * b_key).reshape(kb_ref.shape)
        vb_ref[...] = (scale * b_value).reshape(vb_ref.shape)

    tokens = jnp.concatenate([chunk[...] for chunk in chunks], axis=0)
    product = scale * dot_nn(spread_ref[...], tokens)
    ka_ref[...] = product[:size].reshape(ka_ref.shape)
    va_ref[...] = product[size:].reshape(va_ref.shape)


def adapter_grads(first, sums, sent, rank, per_owner, width, feats):
    count = len(sums)
    rows = sent[0].shape[0]
    chunk = 2 * feats
    steps = width // chunk
    a_spec = pl.BlockSpec((per_owner, rank, chunk), lambda i: (0, 0, i))
    b_spec = pl.BlockSpec((per_owner, rank, feats), lambda i: (0, 0, 0))
    return pl.pallas_call(
        functools.partial(grads_kernel, count, rank, per_owner),
        grid=(steps,),
        in_specs=[pl.BlockSpec(memory_space=pltpu.SMEM)]
        + [pl.BlockSpec(sums[0].shape, lambda i: (0, 0))] * count
        + [pl.BlockSpec((rows, chunk), lambda i: (0, i))] * count
        + [pl.BlockSpec((rows, chunk), lambda i: (0, steps))] * count,
        out_specs=[a_spec, a_spec, b_spec, b_spec],
        out_shape=[
            jax.ShapeDtypeStruct((per_owner, rank, width), f32),
            jax.ShapeDtypeStruct((per_owner, rank, width), f32),
            jax.ShapeDtypeStruct((per_owner, rank, feats), f32),
            jax.ShapeDtypeStruct((per_owner, rank, feats), f32),
        ],
        scratch_shapes=[pltpu.VMEM((2 * per_owner * rank, count * rows), bf16)],
        compiler_params=params(),
        cost_estimate=COST,
        name="adapter_grads",
    )(first, *sums, *sent, *sent)


def swap(values, axis, bit, size):
    return lax.ppermute(values, axis, [(i, i ^ bit) for i in range(size)])


def local(
    tokens, gk, gv, wk, wv, kd, vd, ku, vu, segment_length, segment_tenant, adapter_output_slot
):
    rows, width = tokens.shape
    feats = gk.shape[1]
    adapters, rank, _ = kd.shape
    n_tensor = lax.axis_size("tensor")
    n_dp = lax.axis_size("dp")
    per_owner = adapters // n_dp
    first = (lax.axis_index("dp") * per_owner).astype(jnp.int32).reshape(1)
    in_hbm = functools.partial(pltpu.with_memory_space_constraint, memory_space=pltpu.HBM)
    kd, vd = in_hbm(kd), in_hbm(vd)
    large = [in_hbm(array) for array in (gk, gv, wk, wv)]
    halving = n_tensor == 4

    ahead, early = width * 8 // 16, width * 3 // 16
    first_part, slot_rows = first_products(
        ahead if halving else 0, in_hbm(tokens), large[0], large[1], kd, vd, in_hbm(ku), in_hbm(vu), *large[2:],
        in_hbm(segment_length), in_hbm(segment_tenant), in_hbm(adapter_output_slot),
    )
    tokens, first_part = lax.optimization_barrier((tokens, first_part))
    sent = jnp.concatenate([tokens, gk, gv], axis=1)
    if halving:
        r1a = swap(first_part, "tensor", 1, 4)
        x0b, x2a, x2b, x1 = frozen_blocks(first_part, *large, width, early)
        r1b = swap(x0b, "tensor", 1, 4)
        x2a, r1a = lax.optimization_barrier((x2a, r1a))
        here = jnp.concatenate([r1a[:, :early], r1a[:, ahead:]], axis=1)
        x2a = (x2a + here.astype(f32)).astype(bf16)
        r3a = swap(x2a, "tensor", 2, 4)
        x1, x2a = lax.optimization_barrier((x1, x2a))
        here = jnp.concatenate([r1a[:, early:ahead], r1b], axis=1)
        x2b = (x2b + here.astype(f32)).astype(bf16)
        r3b = swap(x2b, "tensor", 2, 4)
        r4 = swap(x1, "tensor", 1, 4)
        x2b, r3a, x2a = lax.optimization_barrier((x2b, r3a, x2a))
        total = x2a[: 4 * rank, early:].astype(f32) + r3a[: 4 * rank, early:].astype(f32)
        ahead_sum = r3a
    else:
        total = lax.psum(first_part.astype(f32), "tensor")
        term = dot_nt(gk, wk) + dot_nt(gv, wv)
        ahead_sum = lax.psum_scatter(
            term.astype(bf16), "tensor", scatter_dimension=1, tiled=True
        )
    sums = jnp.concatenate([total.astype(bf16), slot_rows], axis=0)

    if n_dp == 4:
        sent_across, sent_core = swap(sent, "dp", 2, 4), swap(sent, "dp", 1, 4)
        pair = jnp.concatenate([sums, swap(sums, "dp", 1, 4)], axis=0)
        pairs = [pair, swap(pair, "dp", 2, 4)]
        size = sums.shape[0]
        all_sums = [two[n * size : (n + 1) * size] for two in pairs for n in (0, 1)]
        all_sent = [sent, sent_core, sent_across, swap(sent_across, "dp", 1, 4)]
    else:
        gathered = lax.all_gather(sent, "dp")
        all_sent = [gathered[i] for i in range(n_dp)]
        gathered = lax.all_gather(sums, "dp")
        all_sums = [gathered[i] for i in range(n_dp)]

    own = add_adapters(halving, ahead_sum, sums, *large, kd, vd, segment_length, segment_tenant)
    grads = adapter_grads(first, all_sums, all_sent, rank, per_owner, width, feats)
    if halving:
        own, *grads = lax.optimization_barrier((own, *grads))
        input_gradient = finish(own, r4, r3b)
    else:
        input_gradient = own.astype(bf16)
    return (input_gradient, *grads)


def solution(mesh):
    placed = (
        P(("group", "dp"), "tensor"),
        P(("group", "dp"), "tensor"),
        P(("group", "dp"), "tensor"),
        P(None, "tensor"),
        P(None, "tensor"),
        P(None, None, "tensor"),
        P(None, None, "tensor"),
        P(None, None, "tensor"),
        P(None, None, "tensor"),
        P(("group", "dp"), None),
        P(("group", "dp"), None),
        P("group"),
    )
    return jax.shard_map(
        local,
        mesh=mesh,
        in_specs=placed,
        out_specs=(
            P(("group", "dp"), "tensor"),
            P(("group", "dp"), None, "tensor"),
            P(("group", "dp"), None, "tensor"),
            P(("group", "dp"), None, "tensor"),
            P(("group", "dp"), None, "tensor"),
        ),
        check_vma=False,
    )
```
